32 devices in a mesh: loc: 16 (over z, y, x), sensor: 2 (over core).
Axes of the slice: x: 2, y: 2, z: 4, core: 2. Of those that a mesh axis runs over, the one named last changes fastest.
Arguments:
- tokens: bfloat16 [2, 2048, 2048], P('sensor', 'loc'), may hold values from -6 to 6
- join_weight: bfloat16 [1, 2, 2048, 2048], P(None, 'sensor'), may hold values from -0.125 to 0.125
- join_gain: bfloat16 [1, 2, 2048], P(None, 'sensor'), may hold values from 0.099609375 to 1.8984375
- moe_gain: bfloat16 [1, 2, 2048], P(None, 'sensor'), may hold values from 0.099609375 to 1.8984375
- w_gate: bfloat16 [1, 32, 2048, 1024], P(None, ('loc', 'sensor')), may hold values from -0.125 to 0.125
- w_up: bfloat16 [1, 32, 2048, 1024], P(None, ('loc', 'sensor')), may hold values from -0.125 to 0.125
- w_down: bfloat16 [1, 32, 1024, 2048], P(None, ('loc', 'sensor')), may hold values from -0.1875 to 0.1875
- expert_ids: int32 [1, 2, 2048, 2], P(None, 'sensor', 'loc'), may hold values from 0 to 31, all different within a row; in each aligned block of 128 rows (0 to 127, 128 to 255, ..., all dimensions but the last counted through in order) at most 12 rows name the same one
- gate_scores: float32 [1, 2, 2048, 2], P(None, 'sensor', 'loc'), may hold values from 0.2 to 1
Outputs:
- layer_output: bfloat16 [2, 2048, 2048], P('sensor', 'loc')
The draws below stay inside these ranges and needn't reach their ends.
Inputs may be any that keep to these rules, and one draw needn't show every extreme that they name: `expert_ids`: take the rows of one layer and sensor in aligned blocks of 128 tokens (the tokens of one index of loc): no expert is named by more than 12 tokens of a block, a bound that some block reaches.
All inputs are finite; a program needn't handle non-finite values.
Results may differ from the reference program's by a relative error of at most 0.012.
Values may be sent and summed in bfloat16 or wider, within the bound.
A program may use at most 128 MiB of HBM per device.

```python
import math
import jax
import jax.numpy as jnp
import numpy as np
from jax import lax

D = 2048
FF = 1024
TOP = 2
LAYERS = 1
TOK_DEV = 128
TOKENS = 2048
EXPERTS = 32
CAP = 12
N_LOC = 16
N_SENSOR = 2


def level_of(key, extent, cuts, least, top_value):
    def one(axis_at, shards_of):
        steps = jax.random.uniform(jax.random.fold_in(jax.random.fold_in(key, 6), axis_at), (shards_of,), jnp.float32, least / len(cuts), top_value / len(cuts))
        return jnp.repeat(jnp.exp(steps), extent[axis_at] // shards_of).reshape((-1,) + (1,) * (len(extent) - axis_at - 1))

    loudness = one(*cuts[0])
    for cut in cuts[1:]:
        loudness = loudness * one(*cut)
    return loudness


def assign_block(key, own, number, rows, number_of, top, limit, lean):
    ranking = jax.random.permutation(key, number_of)
    crowded, usual = load_shares(number_of, rows * top, limit, lean, True), load_shares(number_of, rows * top, limit, lean, False)
    places = jnp.arange(number_of)

    def named(lengths, turn):
        used = int((lengths > 0).sum())
        fixed = max(1, used // 4)
        passed = fixed + (places - fixed + turn * (used - fixed)) % max(1, number_of - fixed)
        return jnp.zeros((number_of,), jnp.int32).at[ranking[jnp.where(places < fixed, places, passed)]].set(jnp.asarray(lengths, jnp.int32))

    lengths = jnp.where(number % 4 == 0, named(crowded, number // 4), named(usual, number - number // 4 - 1))
    mixed = jax.random.permutation(jax.random.fold_in(own, 3), number_of)
    source_of, receiver = mixed[0:number_of // 2 * 2:2], mixed[1:number_of // 2 * 2:2]
    room = jnp.minimum(lengths[source_of] - 1, limit - lengths[receiver]) // 2
    room = jnp.where((source_of == ranking[0]) | (receiver == ranking[0]) | (lengths[receiver] == 0), 0, jnp.maximum(room, 0))
    passed = jax.random.randint(jax.random.fold_in(own, 4), (number_of // 2,), 0, 1 << 20) % (room + 1)
    lengths = lengths.at[source_of].add(-passed).at[receiver].add(passed)
    items = jnp.searchsorted(jnp.cumsum(lengths), jnp.arange(rows * top), side="right").astype(jnp.int32)
    table = items.reshape(top, rows).T
    table = table[jax.random.permutation(jax.random.fold_in(own, 1), rows)]
    turn = jax.random.randint(jax.random.fold_in(own, 2), (rows, 1), 0, top)
    return jnp.take_along_axis(table, (jnp.arange(top)[None, :] + turn) % top, axis=1)


def load_shares(amount, total, bound, lean, full):
    loads = [(1 << 20) // math.isqrt(standing ** lean) + 1 for standing in range(1, amount + 1)]
    largest = bound if full else min(bound, max(-(-total // amount), total * loads[0] // sum(loads)))
    least = 1 if total - largest >= amount - 1 else 0
    holding, rest = [largest] + [least] * (amount - 1), total - largest - least * (amount - 1)
    while rest > 0:
        free = [i for i in range(1, amount) if holding[i] < largest] or [i for i in range(1, amount) if holding[i] < bound]
        mass, left = sum([loads[i] for i in free]), rest
        for i in free:
            extra = min(bound - holding[i], max(1, left * loads[i] // mass), rest)
            holding[i] = holding[i] + extra
            rest = rest - extra
    return np.array(holding)


def normal_values(rng, extent, deviation, most, pieces=(), held_as=jnp.bfloat16):
    loudness = level_of(rng, extent, pieces, -0.22, 0.18) if pieces else 1.0
    array = jax.random.normal(rng, extent, jnp.float32) * deviation * loudness
    return jnp.minimum(jnp.maximum(array, -most), most).astype(held_as)


def setup_inputs(seed: int = 0) -> dict:
    splits = jax.random.split(jax.random.key(seed), 10)
    tokens = normal_values(splits[0], (2, TOKENS, D), 1.0, 6.0, ((0, 2), (1, 16)))
    join_weight = normal_values(splits[1], (LAYERS, 2, D, D), D ** -0.5, 0.125, ((1, 2),))
    join_gain = jnp.clip(1.0 + 0.18 * jax.random.normal(splits[2], (LAYERS, 2, D), jnp.float32), 0.099609375, 1.8984375).astype(jnp.bfloat16)
    moe_gain = jnp.clip(1.0 + 0.18 * jax.random.normal(splits[3], (LAYERS, 2, D), jnp.float32), 0.099609375, 1.8984375).astype(jnp.bfloat16)
    w_gate = normal_values(splits[4], (LAYERS, EXPERTS, D, FF), D ** -0.5, 0.125, ((1, 32),))
    w_up = normal_values(splits[5], (LAYERS, EXPERTS, D, FF), D ** -0.5, 0.125, ((1, 32),))
    w_down = normal_values(splits[6], (LAYERS, EXPERTS, FF, D), FF ** -0.5, 0.1875, ((1, 32),))
    expert_ids_keys = jax.random.split(jax.random.fold_in(splits[7], 1), LAYERS * 2 * TOKENS // TOK_DEV)
    expert_ids_turns = jax.random.permutation(jax.random.fold_in(splits[7], 3), LAYERS * 2 * TOKENS // TOK_DEV)
    expert_ids = jax.vmap(lambda own, number: assign_block(jax.random.fold_in(splits[7], 2), own, number, TOK_DEV, EXPERTS, TOP, CAP, 2))(expert_ids_keys, expert_ids_turns).reshape((LAYERS, 2, TOKENS, TOP))
    gate_scores = jnp.clip(0.2 + 0.8 * jax.random.uniform(splits[8], (LAYERS, 2, TOKENS, TOP), jnp.float32) ** level_of(splits[8], (LAYERS, 2, TOKENS, TOP), ((1, 2), (2, 16)), -0.2, 0.2), 0.2, 1.0)
    return dict(tokens=tokens, join_weight=join_weight, join_gain=join_gain, moe_gain=moe_gain, w_gate=w_gate, w_up=w_up, w_down=w_down, expert_ids=expert_ids, gate_scores=gate_scores)


def norm_rows(values, gain):
    scale = lax.rsqrt(lax.optimization_barrier(jnp.mean(values * values, axis=-1, keepdims=True)) + 1e-05)
    return values * scale * gain.astype(jnp.float32)

def reference(tokens, join_weight, join_gain, moe_gain, w_gate, w_up, w_down, expert_ids, gate_scores):
    stream = tokens
    source_count = N_LOC * N_SENSOR
    entries = TOK_DEV * TOP
    for layer_index in range(LAYERS):
        stream_f = stream.astype(jnp.float32)
        normed = norm_rows(stream_f, join_gain[layer_index][:, None, :]).astype(jnp.bfloat16)
        other_side = normed[::-1]
        projected = jnp.stack([jnp.dot(other_side[side], join_weight[layer_index, side], preferred_element_type=jnp.float32) for side in range(2)])
        joined_rows = (stream_f + projected).astype(jnp.bfloat16)
        mixed_in = norm_rows(joined_rows.astype(jnp.float32), moe_gain[layer_index][:, None, :]).astype(jnp.bfloat16)
        id_blocks = expert_ids[layer_index].reshape(2, N_LOC, entries).transpose(1, 0, 2).reshape(source_count, entries)
        score_blocks = gate_scores[layer_index].reshape(2, N_LOC, entries).transpose(1, 0, 2).reshape(source_count, entries)
        one_hot = (id_blocks[:, :, None] == jnp.arange(EXPERTS, dtype=jnp.int32)[None, None, :]).astype(jnp.int32)
        slot_index = lax.optimization_barrier(jnp.sum((jnp.cumsum(one_hot, axis=1) - one_hot) * one_hot, axis=2)).astype(jnp.int32)
        sources = jnp.broadcast_to(jnp.arange(source_count, dtype=jnp.int32)[:, None], (source_count, entries))
        token_of = jnp.broadcast_to((jnp.arange(entries, dtype=jnp.int32) // TOP)[None, :], (source_count, entries))
        row_of = (sources % 2 * TOKENS + sources // 2 * TOK_DEV + token_of).astype(jnp.int32)
        table = jnp.zeros((EXPERTS, source_count, CAP), jnp.int32).at[id_blocks, sources, slot_index].set(row_of)
        weights_table = jnp.zeros((EXPERTS, source_count, CAP), jnp.float32).at[id_blocks, sources, slot_index].set(score_blocks)
        flat_in = mixed_in.reshape(2 * TOKENS, D)

        def one_expert(total, expert):
            rows_idx = table[expert].reshape(-1)
            picked = flat_in[rows_idx]
            gate_part = jnp.dot(picked, w_gate[layer_index, expert], preferred_element_type=jnp.float32)
            up_part = jnp.dot(picked, w_up[layer_index, expert], preferred_element_type=jnp.float32)
            hidden = (jax.nn.silu(gate_part) * up_part).astype(jnp.bfloat16)
            result = jnp.dot(hidden, w_down[layer_index, expert], preferred_element_type=jnp.float32).astype(jnp.bfloat16)
            scaled = weights_table[expert].reshape(-1, 1) * result.astype(jnp.float32)
            return (total.at[rows_idx].add(scaled), None)
        start = joined_rows.astype(jnp.float32).reshape(2 * TOKENS, D)
        total, unused = lax.scan(one_expert, start, jnp.arange(EXPERTS, dtype=jnp.int32))
        stream = total.astype(jnp.bfloat16).reshape(2, TOKENS, D)
    return stream
```

```python
import jax
import jax.numpy as jnp
from jax import lax
from jax.sharding import PartitionSpec as P


def partner(value, axis, bit):
    return lax.ppermute(value, axis, [(i, i ^ 1 << bit) for i in range(lax.axis_size(axis))])


def norm_rows(values, gain):
    scale = lax.rsqrt(jnp.mean(values * values, axis=-1, keepdims=True) + 1e-05)
    return values * scale * gain.astype(jnp.float32)


def expert_block(received, gate_w, up_w, down_w):
    rows = received.reshape(-1, received.shape[-1])
    gate_part = jnp.dot(rows, gate_w, preferred_element_type=jnp.float32)
    up_part = jnp.dot(rows, up_w, preferred_element_type=jnp.float32)
    hidden = (jax.nn.silu(gate_part) * up_part).astype(jnp.bfloat16)
    result = jnp.dot(hidden, down_w, preferred_element_type=jnp.float32).astype(jnp.bfloat16)
    return result.reshape(received.shape)


def body(tokens, join_weight, join_gain, moe_gain, w_gate, w_up, w_down, expert_ids, gate_scores):
    loc_count = lax.axis_size("loc")
    sensor_count = lax.axis_size("sensor")
    stream = tokens[0]
    tok_rows = stream.shape[0]
    feature_width = stream.shape[1]
    top_count = expert_ids.shape[3]
    expert_total = loc_count * sensor_count
    capacity = max(2, (3 * top_count * tok_rows + 2 * expert_total - 1) // (2 * expert_total))
    slots = expert_total * capacity
    own_gain = join_gain[0, 0]
    other_rows, other_gain = partner((stream, own_gain), "sensor", 0)
    normed = norm_rows(other_rows.astype(jnp.float32), other_gain).astype(jnp.bfloat16)
    projected = jnp.dot(normed, join_weight[0, 0], preferred_element_type=jnp.float32)
    joined_rows = (stream.astype(jnp.float32) + projected).astype(jnp.bfloat16)
    mixed_in = norm_rows(joined_rows.astype(jnp.float32), moe_gain[0, 0]).astype(jnp.bfloat16)
    ids = expert_ids[0, 0]
    experts = jnp.arange(expert_total, dtype=jnp.int32)
    one_hot = (ids[:, :, None] == experts[None, None, :]).astype(jnp.float32)
    named = jnp.sum(one_hot, axis=1)
    before = jnp.tril(jnp.ones((tok_rows, tok_rows), jnp.float32), -1)
    earlier = jnp.dot(before, named)
    slot_index = jnp.sum(earlier[:, None, :] * one_hot, axis=2).astype(jnp.int32)
    position = ids * capacity + slot_index
    place = position[:, :, None] == jnp.arange(slots, dtype=jnp.int32)[None, None, :]
    spread = jnp.any(place, axis=1).astype(jnp.bfloat16)
    weights = jnp.sum(jnp.where(place, gate_scores[0, 0][:, :, None], 0.0), axis=1)
    high = weights.astype(jnp.bfloat16)
    low = (weights - high.astype(jnp.float32)).astype(jnp.bfloat16)
    send_rows = lax.dot_general(
        spread, mixed_in, (((0,), (0,)), ((), ())), preferred_element_type=jnp.float32
    ).astype(jnp.bfloat16)
    send_rows = send_rows.reshape(expert_total, capacity, feature_width)
    answered = expert_block(
        lax.all_to_all(send_rows, ("loc", "sensor"), split_axis=0, concat_axis=0, tiled=True),
        w_gate[0, 0],
        w_up[0, 0],
        w_down[0, 0],
    )
    returned = lax.all_to_all(answered, ("loc", "sensor"), split_axis=0, concat_axis=0, tiled=True)
    returned = returned.reshape(slots, feature_width)
    combined = jnp.dot(
        jnp.concatenate([high, low], axis=1),
        jnp.concatenate([returned, returned], axis=0),
        preferred_element_type=jnp.float32,
    )
    stream = (joined_rows.astype(jnp.float32) + combined).astype(jnp.bfloat16)
    return stream[None]


def solution(mesh):
    placed = (
        P("sensor", "loc", None),
        P(None, "sensor", None, None),
        P(None, "sensor", None),
        P(None, "sensor", None),
        P(None, ("loc", "sensor"), None, None),
        P(None, ("loc", "sensor"), None, None),
        P(None, ("loc", "sensor"), None, None),
        P(None, "sensor", "loc", None),
        P(None, "sensor", "loc", None),
    )
    return jax.shard_map(
        body, mesh=mesh, in_specs=placed, out_specs=P("sensor", "loc", None), check_vma=False
    )
```

```python
import functools
import math
import jax
import jax.numpy as jnp
from jax import lax
from jax.experimental import pallas as pl
from jax.experimental.pallas import tpu as pltpu
from jax.sharding import PartitionSpec as P

MESH = pl.DeviceIdType.MESH


def partner(value, axis, bit):
    return lax.ppermute(value, axis, [(i, i ^ 1 << bit) for i in range(lax.axis_size(axis))])


def norm_rows(values, gain):
    scale = lax.rsqrt(jnp.mean(values * values, axis=-1, keepdims=True) + 1e-05)
    return values * scale * gain.astype(jnp.float32)


def dot(a, b):
    return jnp.dot(a, b, preferred_element_type=jnp.float32)


def kernel(
    dims,
    mixed_ref,
    joined_ref,
    spread_ref,
    weight_ref,
    pack_ref,
    unpack_ref,
    gate_hbm,
    up_hbm,
    down_hbm,
    out_ref,
    gate_ref,
    up_ref,
    down_ref,
    sent,
    got,
    answer,
    back,
    stack,
    rows,
    hidden,
    acc,
    load_sems,
    sent_sems,
    got_sems,
    answer_sems,
    back_sems,
):
    planes, members, sensors, pieces = dims
    total = planes * members
    piece = stack.shape[1]
    plane_rows = rows.shape[0]
    slab = sent.shape[1]
    width = rows.shape[1]
    hidden_width = hidden.shape[1]
    me = lax.axis_index("loc") * sensors + lax.axis_index("sensor")
    my_plane = me // members
    my_place = me % members
    half = planes // 2
    my_half = my_plane // half

    def device(index):
        return (index // sensors, index % sensors)

    loads = [
        pltpu.make_async_copy(src, dst, load_sems.at[i])
        for i, (src, dst) in enumerate(
            ((gate_hbm, gate_ref), (up_hbm, up_ref), (down_hbm, down_ref))
        )
    ]
    for load in loads:
        load.start()

    barrier = pltpu.get_barrier_semaphore()

    def greet(i, _):
        other = lax.rem(me + i, total)
        pl.semaphore_signal(barrier, inc=1, device_id=device(other), device_id_type=MESH)
        return _

    lax.fori_loop(1, total, greet, 0)

    def far(k):
        return (1 - my_half) * half + (my_plane + k) % half

    def near(k):
        return my_half * half + (my_plane + k) % half

    def plane_out(step):
        return jnp.where(step < half, far(step), near(step))

    def plane_in(step):
        return jnp.where(step < half, near(step), far(step))

    def pack(values, target, plane):
        for c in range(pieces):
            stack[c * plane_rows : (c + 1) * plane_rows, :] = values[:, c * piece : (c + 1) * piece]
        packed = dot(pack_ref[...], stack[...]).astype(jnp.bfloat16)
        target[pl.ds(plane * members, members)] = packed.reshape(members, slab, piece)

    def unpack(source, plane):
        values = source[pl.ds(plane * members, members)].reshape(members * slab, piece)
        return dot(unpack_ref[...], values).astype(jnp.bfloat16)

    def copy(source, target, send_sems, recv_sems, other, landing):
        return pltpu.make_async_remote_copy(
            src_ref=source.at[other],
            dst_ref=target.at[landing],
            send_sem=send_sems.at[other],
            recv_sem=recv_sems.at[landing],
            device_id=device(other),
            device_id_type=MESH,
        )

    def send_plane(source, target, send_sems, recv_sems, plane):
        def one(i, _):
            other = plane * members + lax.rem(my_place + i, members)

            @pl.when(other != me)
            def _send():
                copy(source, target, send_sems, recv_sems, other, me).start()

            @pl.when(other == me)
            def _keep():
                target[me] = source[me]

            return _

        lax.fori_loop(0, members, one, 0)

    def await_plane(source, target, send_sems, recv_sems, plane):
        def one(i, _):
            other = plane * members + lax.rem(my_place + i, members)

            @pl.when(other != me)
            def _wait():
                copy(source, target, send_sems, recv_sems, other, other).wait_recv()

            return _

        lax.fori_loop(0, members, one, 0)

    def dispatch(step, _):
        plane = plane_out(step)
        picked = dot(spread_ref[plane], mixed_ref[...]).astype(jnp.bfloat16)
        pack(picked, sent, plane)

        @pl.when(step == 0)
        def _enter():
            pl.semaphore_wait(barrier, total - 1)

        send_plane(sent, got, sent_sems, got_sems, plane)
        return _

    lax.fori_loop(0, planes, dispatch, 0)

    for load in loads:
        load.wait()

    tile = min(256, hidden_width)
    down_tile = min(512, width)

    def experts(step, _):
        plane = plane_in(step)
        await_plane(sent, got, sent_sems, got_sems, plane)
        stack[...] = unpack(got, plane)
        for c in range(pieces):
            rows[:, c * piece : (c + 1) * piece] = stack[c * plane_rows : (c + 1) * plane_rows, :]

        def hide(j, _):
            part = pl.ds(pl.multiple_of(j * tile, tile), tile)
            gate_part = dot(rows[...], gate_ref[:, part])
            up_part = dot(rows[...], up_ref[:, part])
            value = gate_part / (1.0 + jnp.exp(-gate_part)) * up_part
            hidden[:, part] = value.astype(jnp.bfloat16)
            return _

        lax.fori_loop(0, hidden_width // tile, hide, 0)

        def lower(j, _):
            part = pl.ds(pl.multiple_of(j * down_tile, down_tile), down_tile)
            rows[:, part] = dot(hidden[...], down_ref[:, part]).astype(jnp.bfloat16)
            return _

        lax.fori_loop(0, width // down_tile, lower, 0)
        pack(rows, answer, plane)
        send_plane(answer, back, answer_sems, back_sems, plane)
        return _

    lax.fori_loop(0, planes, experts, 0)

    acc[...] = joined_ref[...].astype(jnp.float32)

    def combine(step, _):
        plane = plane_in(step)
        await_plane(answer, back, answer_sems, back_sems, plane)
        stack[...] = unpack(back, plane)
        for c in range(pieces):
            values = stack[c * plane_rows : (c + 1) * plane_rows, :]
            cols = slice(c * piece, (c + 1) * piece)
            acc[:, cols] += dot(weight_ref[plane, 0], values) + dot(weight_ref[plane, 1], values)
        return _

    lax.fori_loop(0, planes, combine, 0)
    out_ref[...] = acc[...].astype(jnp.bfloat16)

    def finish(i, _):
        other = lax.rem(me + i, total)
        copy(sent, got, sent_sems, got_sems, other, me).wait_send()
        copy(answer, back, answer_sems, back_sems, other, me).wait_send()
        return _

    lax.fori_loop(1, total, finish, 0)


def body(tokens, join_weight, join_gain, moe_gain, w_gate, w_up, w_down, expert_ids, gate_scores):
    loc_count = lax.axis_size("loc")
    sensor_count = lax.axis_size("sensor")
    stream = tokens[0]
    tok_rows = stream.shape[0]
    width = stream.shape[1]
    hidden_width = w_gate.shape[3]
    top_count = expert_ids.shape[3]
    expert_total = loc_count * sensor_count
    capacity = max(2, (3 * top_count * tok_rows + 2 * expert_total - 1) // (2 * expert_total))
    planes = 4
    members = expert_total // planes
    plane_rows = members * capacity
    pieces = 16 // math.gcd(16, capacity)
    piece = width // pieces
    slab = pieces * capacity
    own_gain = join_gain[0, 0]
    other_rows, other_gain = partner((stream, own_gain), "sensor", 0)
    normed = norm_rows(other_rows.astype(jnp.float32), other_gain).astype(jnp.bfloat16)
    projected = jnp.dot(normed, join_weight[0, 0], preferred_element_type=jnp.float32)
    joined_rows = (stream.astype(jnp.float32) + projected).astype(jnp.bfloat16)
    mixed_in = norm_rows(joined_rows.astype(jnp.float32), moe_gain[0, 0]).astype(jnp.bfloat16)
    ids = expert_ids[0, 0]
    scores = gate_scores[0, 0]
    experts = jnp.arange(expert_total, dtype=jnp.int32)
    one_hot = (ids[:, :, None] == experts[None, None, :]).astype(jnp.float32)
    named = jnp.sum(one_hot, axis=1)
    before = jnp.tril(jnp.ones((tok_rows, tok_rows), jnp.float32), -1)
    earlier = jnp.dot(before, named)
    slot_index = jnp.sum(earlier[:, None, :] * one_hot, axis=2).astype(jnp.int32)
    position = ids * capacity + slot_index
    slots = jnp.arange(expert_total * capacity, dtype=jnp.int32).reshape(planes, 1, plane_rows)
    place = [position[:, k][None, :, None] == slots for k in range(top_count)]
    weights = sum(jnp.where(place[k], scores[:, k][None, :, None], 0.0) for k in range(top_count))
    high = weights.astype(jnp.bfloat16)
    low = (weights - high.astype(jnp.float32)).astype(jnp.bfloat16)
    weights = jnp.stack([high, low], axis=1)
    slots = slots.reshape(planes, plane_rows, 1)
    spread = sum(
        (slots == position[:, k][None, None, :]).astype(jnp.bfloat16) for k in range(top_count)
    )
    line = jnp.arange(members * slab, dtype=jnp.int32)
    place_of = (line // capacity) % pieces * plane_rows + line // slab * capacity + line % capacity
    pack = (place_of[:, None] == line[None, :]).astype(jnp.bfloat16)
    unpack = (line[:, None] == place_of[None, :]).astype(jnp.bfloat16)
    vmem = pl.BlockSpec(memory_space=pltpu.VMEM)
    hbm = pl.BlockSpec(memory_space=pl.ANY)
    box = pltpu.VMEM((expert_total, slab, piece), jnp.bfloat16)
    out = pl.pallas_call(
        functools.partial(kernel, (planes, members, sensor_count, pieces)),
        out_shape=jax.ShapeDtypeStruct((tok_rows, width), jnp.bfloat16),
        in_specs=[vmem] * 6 + [hbm] * 3,
        out_specs=vmem,
        scratch_shapes=[
            pltpu.VMEM((width, hidden_width), jnp.bfloat16),
            pltpu.VMEM((width, hidden_width), jnp.bfloat16),
            pltpu.VMEM((hidden_width, width), jnp.bfloat16),
            box,
            box,
            box,
            box,
            pltpu.VMEM((pieces * plane_rows, piece), jnp.bfloat16),
            pltpu.VMEM((plane_rows, width), jnp.bfloat16),
            pltpu.VMEM((plane_rows, hidden_width), jnp.bfloat16),
            pltpu.VMEM((tok_rows, width), jnp.float32),
            pltpu.SemaphoreType.DMA((3,)),
            pltpu.SemaphoreType.DMA((expert_total,)),
            pltpu.SemaphoreType.DMA((expert_total,)),
            pltpu.SemaphoreType.DMA((expert_total,)),
            pltpu.SemaphoreType.DMA((expert_total,)),
        ],
        compiler_params=pltpu.CompilerParams(
            collective_id=0, has_side_effects=True, vmem_limit_bytes=52 * 1024 * 1024
        ),
    )(
        mixed_in,
        joined_rows,
        spread,
        weights,
        pack,
        unpack,
        w_gate[0, 0],
        w_up[0, 0],
        w_down[0, 0],
    )
    return out[None]


def solution(mesh):
    placed = (
        P("sensor", "loc", None),
        P(None, "sensor", None, None),
        P(None, "sensor", None),
        P(None, "sensor", None),
        P(None, ("loc", "sensor"), None, None),
        P(None, ("loc", "sensor"), None, None),
        P(None, ("loc", "sensor"), None, None),
        P(None, "sensor", "loc", None),
        P(None, "sensor", "loc", None),
    )
    return jax.shard_map(
        body, mesh=mesh, in_specs=placed, out_specs=P("sensor", "loc", None), check_vma=False
    )
```

```python
import functools
import math
import jax
import jax.numpy as jnp
from jax import lax
from jax.experimental import pallas as pl
from jax.experimental.pallas import tpu as pltpu
from jax.sharding import PartitionSpec as P

MESH = pl.DeviceIdType.MESH


def partner(value, axis, bit):
    return lax.ppermute(value, axis, [(i, i ^ 1 << bit) for i in range(lax.axis_size(axis))])


def norm_rows(values, gain):
    scale = lax.rsqrt(jnp.mean(values * values, axis=-1, keepdims=True) + 1e-05)
    return values * scale * gain.astype(jnp.float32)


def dot(a, b):
    return jnp.dot(a, b, preferred_element_type=jnp.float32)


def kernel(
    dims,
    mixed_ref,
    joined_ref,
    spread_ref,
    weight_ref,
    pack_ref,
    unpack_ref,
    gate_hbm,
    up_hbm,
    down_hbm,
    out_ref,
    gate_ref,
    up_ref,
    down_ref,
    foreign,
    partial,
    partial_in,
    sent,
    got,
    answer,
    back,
    stack,
    rows,
    hidden,
    acc,
    load_sems,
    block_sems,
    foreign_sems,
    partial_sems,
    partial_in_sems,
    sent_sems,
    got_sems,
    answer_sems,
    back_sems,
):
    members, sensors, pieces = dims
    mates = 2 * members
    total = 2 * mates
    chunks, _, chunk = mixed_ref.shape
    piece = stack.shape[1]
    slab = sent.shape[3]
    plane_rows = rows.shape[0] // 2
    hidden_width = hidden.shape[1]
    me = lax.axis_index("loc") * sensors + lax.axis_index("sensor")
    base = me // mates * mates
    mine = me % mates
    my_plane = mine // members
    my_place = mine % members
    partner_device = lax.rem(me + mates, total)

    def device(index):
        return (index // sensors, index % sensors)

    loads = [
        pltpu.make_async_copy(src, dst, load_sems.at[i])
        for i, (src, dst) in enumerate(
            ((gate_hbm, gate_ref), (up_hbm, up_ref), (down_hbm, down_ref))
        )
    ]
    for load in loads:
        load.start()

    barrier = pltpu.get_barrier_semaphore()
    pl.semaphore_signal(barrier, inc=1, device_id=device(partner_device), device_id_type=MESH)

    def greet(i, _):
        other = base + lax.rem(mine + i, mates)
        pl.semaphore_signal(barrier, inc=1, device_id=device(other), device_id_type=MESH)
        return _

    lax.fori_loop(1, mates, greet, 0)
    pl.semaphore_wait(barrier, mates)

    def across(source, target, send_sems, recv_sems, c):
        return pltpu.make_async_remote_copy(
            src_ref=source.at[c],
            dst_ref=target.at[c],
            send_sem=send_sems.at[c],
            recv_sem=recv_sems.at[c],
            device_id=device(partner_device),
            device_id_type=MESH,
        )

    def copy(way, q, c, other, landing):
        source, target, send_sems, recv_sems = way
        return pltpu.make_async_remote_copy(
            src_ref=source.at[q, c, other],
            dst_ref=target.at[q, c, landing],
            send_sem=send_sems.at[q, c, other],
            recv_sem=recv_sems.at[q, c, landing],
            device_id=device(base + other),
            device_id_type=MESH,
        )

    out_way = (sent, got, sent_sems, got_sems)
    home_way = (answer, back, answer_sems, back_sems)

    def send_plane(way, q, c, plane):
        def one(i, _):
            other = plane * members + lax.rem(my_place + i, members)

            @pl.when(other != mine)
            def _send():
                copy(way, q, c, other, mine).start()

            @pl.when(other == mine)
            def _keep():
                way[1][q, c, mine] = way[0][q, c, mine]

            return _

        lax.fori_loop(0, members, one, 0)

    def await_all(way, q, c):
        def one(i, _):
            other = lax.rem(mine + i, mates)
            copy(way, q, c, other, other).wait_recv()
            return _

        lax.fori_loop(1, mates, one, 0)

    def pack(values, way, q, c, plane):
        for i in range(pieces):
            stack[i * plane_rows : (i + 1) * plane_rows, :] = values[:, i * piece : (i + 1) * piece]
        packed = dot(pack_ref[...], stack[...]).astype(jnp.bfloat16)
        way[0][q, c, pl.ds(plane * members, members)] = packed.reshape(members, slab, piece)
        send_plane(way, q, c, plane)

    def unpack(way, q, c, plane):
        values = way[1][q, c, pl.ds(plane * members, members)].reshape(members * slab, piece)
        stack[...] = dot(unpack_ref[...], values).astype(jnp.bfloat16)

    def dispatch(q, source, c):
        def one(step, _):
            plane = lax.rem(my_plane + 1 + step, 2)
            picked = dot(spread_ref[q, plane], source[c]).astype(jnp.bfloat16)
            pack(picked, out_way, q, c, plane)
            return _

        lax.fori_loop(0, 2, one, 0)

    tile = min(256, hidden_width)

    def plane_slice(plane):
        return pl.ds(pl.multiple_of(plane * plane_rows, 16), plane_rows)

    def experts(q):
        for c in range(chunks):
            await_all(out_way, q, c)

            def one(plane, _, c=c):
                unpack(out_way, q, c, plane)
                for i in range(pieces):
                    cols = slice(c * chunk + i * piece, c * chunk + (i + 1) * piece)
                    rows[plane_slice(plane), cols] = stack[i * plane_rows : (i + 1) * plane_rows, :]
                return _

            lax.fori_loop(0, 2, one, 0)

        def hide(j, _):
            part = pl.ds(pl.multiple_of(j * tile, tile), tile)
            gate_part = dot(rows[...], gate_ref[:, part])
            up_part = dot(rows[...], up_ref[:, part])
            value = gate_part / (1.0 + jnp.exp(-gate_part)) * up_part
            hidden[:, part] = value.astype(jnp.bfloat16)
            return _

        lax.fori_loop(0, hidden_width // tile, hide, 0)
        for c in range(chunks):
            cols = slice(c * chunk, (c + 1) * chunk)
            rows[:, cols] = dot(hidden[...], down_ref[:, cols]).astype(jnp.bfloat16)

            def one(step, _, c=c, cols=cols):
                plane = lax.rem(my_plane + 1 + step, 2)
                pack(rows[plane_slice(plane), cols], home_way, q, c, plane)
                return _

            lax.fori_loop(0, 2, one, 0)

    def combine(q, c):
        await_all(home_way, q, c)

        def one(plane, _):
            unpack(home_way, q, c, plane)
            for i in range(pieces):
                values = stack[i * plane_rows : (i + 1) * plane_rows, :]
                cols = slice(i * piece, (i + 1) * piece)
                acc[c, :, cols] += dot(weight_ref[q, plane, 0], values) + dot(
                    weight_ref[q, plane, 1], values
                )
            return _

        lax.fori_loop(0, 2, one, 0)

    for c in range(chunks):
        across(mixed_ref, foreign, block_sems, foreign_sems, c).start()
    for c in range(chunks):
        dispatch(0, mixed_ref, c)
    for c in range(chunks):
        across(mixed_ref, foreign, block_sems, foreign_sems, c).wait_recv()
        dispatch(1, foreign, c)
        if c == max(0, chunks - 2):
            for load in loads:
                load.wait()
            experts(0)
    experts(1)
    for c in range(chunks):
        acc[c] = jnp.zeros_like(acc[c])
        combine(1, c)
        partial[c] = acc[c].astype(jnp.bfloat16)
        across(partial, partial_in, partial_sems, partial_in_sems, c).start()
    for c in range(chunks):
        acc[c] = joined_ref[:, c * chunk : (c + 1) * chunk].astype(jnp.float32)
        combine(0, c)
    for c in range(chunks):
        across(partial, partial_in, partial_sems, partial_in_sems, c).wait_recv()
        out_ref[:, c * chunk : (c + 1) * chunk] = (
            acc[c] + partial_in[c].astype(jnp.float32)
        ).astype(jnp.bfloat16)

    def finish(i, _):
        other = lax.rem(mine + i, mates)
        for q in range(2):
            for c in range(chunks):
                copy(out_way, q, c, other, mine).wait_send()
                copy(home_way, q, c, other, mine).wait_send()
        return _

    lax.fori_loop(1, mates, finish, 0)
    for c in range(chunks):
        across(mixed_ref, foreign, block_sems, foreign_sems, c).wait_send()
        across(partial, partial_in, partial_sems, partial_in_sems, c).wait_send()


def body(tokens, join_weight, join_gain, moe_gain, w_gate, w_up, w_down, expert_ids, gate_scores):
    loc_count = lax.axis_size("loc")
    sensor_count = lax.axis_size("sensor")
    stream = tokens[0]
    tok_rows = stream.shape[0]
    width = stream.shape[1]
    hidden_width = w_gate.shape[3]
    top_count = expert_ids.shape[3]
    expert_total = loc_count * sensor_count
    capacity = max(2, (3 * top_count * tok_rows + 2 * expert_total - 1) // (2 * expert_total))
    planes = 4
    mates = expert_total // 2
    members = expert_total // planes
    plane_rows = members * capacity
    pieces = 16 // math.gcd(16, capacity)
    chunks = max(1, min(2, width // (128 * pieces)))
    chunk = width // chunks
    piece = chunk // pieces
    slab = pieces * capacity
    turn = [(i, (i + loc_count // 2) % loc_count) for i in range(loc_count)]
    ids = expert_ids[0, 0]
    scores = gate_scores[0, 0]
    route = (
        jnp.stack([ids, lax.ppermute(ids, "loc", turn)]),
        jnp.stack([scores, lax.ppermute(scores, "loc", turn)]),
    )
    own_gain = join_gain[0, 0]
    other_rows, other_gain = partner((stream, own_gain), "sensor", 0)
    normed = norm_rows(other_rows.astype(jnp.float32), other_gain).astype(jnp.bfloat16)
    projected = jnp.dot(normed, join_weight[0, 0], preferred_element_type=jnp.float32)
    joined_rows = (stream.astype(jnp.float32) + projected).astype(jnp.bfloat16)
    mixed_in = norm_rows(joined_rows.astype(jnp.float32), moe_gain[0, 0]).astype(jnp.bfloat16)
    mixed_in = mixed_in.reshape(tok_rows, chunks, chunk).transpose(1, 0, 2)
    ids, scores = route
    experts = jnp.arange(expert_total, dtype=jnp.int32)
    one_hot = (ids[:, :, :, None] == experts).astype(jnp.float32)
    named = jnp.sum(one_hot, axis=2)
    before = jnp.tril(jnp.ones((tok_rows, tok_rows), jnp.float32), -1)
    earlier = jnp.einsum("ts,qse->qte", before, named)
    slot_index = jnp.sum(earlier[:, :, None, :] * one_hot, axis=3).astype(jnp.int32)
    position = ids * capacity + slot_index
    first = lax.axis_index("loc") // (loc_count // 2) * (mates * capacity)
    slots = first + jnp.arange(mates * capacity, dtype=jnp.int32).reshape(2, 1, plane_rows)
    weights = sum(
        jnp.where(position[:, None, :, k, None] == slots, scores[:, None, :, k, None], 0.0)
        for k in range(top_count)
    )
    high = weights.astype(jnp.bfloat16)
    low = (weights - high.astype(jnp.float32)).astype(jnp.bfloat16)
    weights = jnp.stack([high, low], axis=2)
    slots = slots.reshape(2, plane_rows, 1)
    spread = sum(
        (slots == position[:, None, None, :, k]).astype(jnp.bfloat16) for k in range(top_count)
    )
    line = jnp.arange(members * slab, dtype=jnp.int32)
    place_of = (line // capacity) % pieces * plane_rows + line // slab * capacity + line % capacity
    pack = (place_of[:, None] == line[None, :]).astype(jnp.bfloat16)
    unpack = (line[:, None] == place_of[None, :]).astype(jnp.bfloat16)
    vmem = pl.BlockSpec(memory_space=pltpu.VMEM)
    hbm = pl.BlockSpec(memory_space=pl.ANY)
    box = pltpu.VMEM((2, chunks, mates, slab, piece), jnp.bfloat16)
    whole = pltpu.VMEM((chunks, tok_rows, chunk), jnp.bfloat16)
    pair = pltpu.SemaphoreType.DMA((chunks,))
    each = pltpu.SemaphoreType.DMA((2, chunks, mates))
    out = pl.pallas_call(
        functools.partial(kernel, (members, sensor_count, pieces)),
        out_shape=jax.ShapeDtypeStruct((tok_rows, width), jnp.bfloat16),
        in_specs=[vmem] * 6 + [hbm] * 3,
        out_specs=vmem,
        scratch_shapes=[
            pltpu.VMEM((width, hidden_width), jnp.bfloat16),
            pltpu.VMEM((width, hidden_width), jnp.bfloat16),
            pltpu.VMEM((hidden_width, width), jnp.bfloat16),
            whole,
            whole,
            whole,
            box,
            box,
            box,
            box,
            pltpu.VMEM((pieces * plane_rows, piece), jnp.bfloat16),
            pltpu.VMEM((2 * plane_rows, width), jnp.bfloat16),
            pltpu.VMEM((2 * plane_rows, hidden_width), jnp.bfloat16),
            pltpu.VMEM((chunks, tok_rows, chunk), jnp.float32),
            pltpu.SemaphoreType.DMA((3,)),
            pair,
            pair,
            pair,
            pair,
            each,
            each,
            each,
            each,
        ],
        compiler_params=pltpu.CompilerParams(
            collective_id=0, has_side_effects=True, vmem_limit_bytes=52 * 1024 * 1024
        ),
    )(
        mixed_in,
        joined_rows,
        spread,
        weights,
        pack,
        unpack,
        w_gate[0, 0],
        w_up[0, 0],
        w_down[0, 0],
    )
    return out[None]


def solution(mesh):
    placed = (
        P("sensor", "loc", None),
        P(None, "sensor", None, None),
        P(None, "sensor", None),
        P(None, "sensor", None),
        P(None, ("loc", "sensor"), None, None),
        P(None, ("loc", "sensor"), None, None),
        P(None, ("loc", "sensor"), None, None),
        P(None, "sensor", "loc", None),
        P(None, "sensor", "loc", None),
    )
    return jax.shard_map(
        body, mesh=mesh, in_specs=placed, out_specs=P("sensor", "loc", None), check_vma=False
    )
```

```python
import functools
import math
import jax
import jax.numpy as jnp
from jax import lax
from jax.experimental import pallas as pl
from jax.experimental.pallas import tpu as pltpu
from jax.sharding import PartitionSpec as P

MESH = pl.DeviceIdType.MESH


def norm_rows(values, gain):
    scale = lax.rsqrt(jnp.mean(values * values, axis=-1, keepdims=True) + 1e-05)
    return values * scale * gain.astype(jnp.float32)


def dot(a, b):
    return jnp.dot(a, b, preferred_element_type=jnp.float32)


def kernel(
    dims,
    stream_ref,
    join_gain_ref,
    moe_gain_ref,
    ids_ref,
    scores_ref,
    pack_ref,
    unpack_ref,
    join_hbm,
    gate_hbm,
    up_hbm,
    down_hbm,
    out_ref,
    join_ref,
    gate_ref,
    up_ref,
    down_ref,
    sent,
    got,
    answer,
    back,
    stack,
    rows,
    hidden,
    acc,
    normed,
    normed_in,
    joined,
    mixed,
    spread,
    weight,
    load_sems,
    swap_sems,
    sent_sems,
    got_sems,
    answer_sems,
    back_sems,
):
    planes, members, sensors, pieces, capacity = dims
    total = planes * members
    piece = stack.shape[1]
    plane_rows = rows.shape[0]
    slab = sent.shape[1]
    width = rows.shape[1]
    hidden_width = hidden.shape[1]
    me = lax.axis_index("loc") * sensors + lax.axis_index("sensor")
    my_plane = me // members
    my_place = me % members
    half = planes // 2
    my_half = my_plane // half

    def device(index):
        return (index // sensors, index % sensors)

    join_load = pltpu.make_async_copy(join_hbm, join_ref, load_sems.at[3])
    join_load.start()
    loads = [
        pltpu.make_async_copy(src, dst, load_sems.at[i])
        for i, (src, dst) in enumerate(
            ((gate_hbm, gate_ref), (up_hbm, up_ref), (down_hbm, down_ref))
        )
    ]

    barrier = pltpu.get_barrier_semaphore()

    def greet(i, _):
        other = lax.rem(me + i, total)
        pl.semaphore_signal(barrier, inc=1, device_id=device(other), device_id_type=MESH)
        return _

    lax.fori_loop(1, total, greet, 0)

    normed[...] = norm_rows(stream_ref[...].astype(jnp.float32), join_gain_ref[...]).astype(
        jnp.bfloat16
    )
    pl.semaphore_wait(barrier, total - 1)
    swap = pltpu.make_async_remote_copy(
        src_ref=normed,
        dst_ref=normed_in,
        send_sem=swap_sems.at[0],
        recv_sem=swap_sems.at[1],
        device_id=(lax.axis_index("loc"), 1 - lax.axis_index("sensor")),
        device_id_type=MESH,
    )
    swap.start()

    tok_rows = stream_ref.shape[0]
    ids = ids_ref[...]
    scores = scores_ref[...]
    top_count = ids.shape[1]
    expert = lax.broadcasted_iota(jnp.int32, (tok_rows, total), 1)
    chosen = [(ids[:, k : k + 1] == expert).astype(jnp.float32) for k in range(top_count)]
    lower_rows = lax.broadcasted_iota(jnp.int32, (tok_rows, tok_rows), 0)
    lower_cols = lax.broadcasted_iota(jnp.int32, (tok_rows, tok_rows), 1)
    before = (lower_cols < lower_rows).astype(jnp.float32).astype(jnp.bfloat16)
    earlier = dot(before, sum(chosen).astype(jnp.bfloat16))
    position = [
        ids[:, k : k + 1] * capacity
        + jnp.sum(earlier * chosen[k], axis=1, keepdims=True).astype(jnp.int32)
        for k in range(top_count)
    ]
    for plane in range(planes):
        slot = plane * plane_rows + lax.broadcasted_iota(jnp.int32, (tok_rows, plane_rows), 1)
        taken = [position[k] == slot for k in range(top_count)]
        spread[plane] = sum(jnp.where(t, 1.0, 0.0) for t in taken).astype(jnp.bfloat16)
        value = sum(jnp.where(taken[k], scores[:, k : k + 1], 0.0) for k in range(top_count))
        high = value.astype(jnp.bfloat16)
        weight[plane, 0] = high
        weight[plane, 1] = (value - high.astype(jnp.float32)).astype(jnp.bfloat16)

    swap.wait()
    join_load.wait()
    for load in loads:
        load.start()
    join_tile = min(512, width)

    def join(j, _):
        part = pl.ds(pl.multiple_of(j * join_tile, join_tile), join_tile)
        value = stream_ref[:, part].astype(jnp.float32) + dot(normed_in[...], join_ref[:, part])
        joined[:, part] = value.astype(jnp.bfloat16)
        return _

    lax.fori_loop(0, width // join_tile, join, 0)
    mixed[...] = norm_rows(joined[...].astype(jnp.float32), moe_gain_ref[...]).astype(jnp.bfloat16)

    def far(k):
        return (1 - my_half) * half + (my_plane + k) % half

    def near(k):
        return my_half * half + (my_plane + k) % half

    def plane_out(step):
        return jnp.where(step < half, far(step), near(step))

    def plane_in(step):
        return jnp.where(step % 2 == 0, near(step // 2), far(step // 2))

    def pack(values, target, plane):
        for c in range(pieces):
            stack[c * plane_rows : (c + 1) * plane_rows, :] = values[:, c * piece : (c + 1) * piece]
        packed = dot(pack_ref[...], stack[...]).astype(jnp.bfloat16)
        target[pl.ds(plane * members, members)] = packed.reshape(members, slab, piece)

    def unpack(source, plane):
        values = source[pl.ds(plane * members, members)].reshape(members * slab, piece)
        return dot(unpack_ref[...], values).astype(jnp.bfloat16)

    def copy(source, target, send_sems, recv_sems, other, landing):
        return pltpu.make_async_remote_copy(
            src_ref=source.at[other],
            dst_ref=target.at[landing],
            send_sem=send_sems.at[other],
            recv_sem=recv_sems.at[landing],
            device_id=device(other),
            device_id_type=MESH,
        )

    def send_plane(source, target, send_sems, recv_sems, plane):
        def one(i, _):
            other = plane * members + lax.rem(my_place + i, members)

            @pl.when(other != me)
            def _send():
                copy(source, target, send_sems, recv_sems, other, me).start()

            @pl.when(other == me)
            def _keep():
                target[me] = source[me]

            return _

        lax.fori_loop(0, members, one, 0)

    def await_plane(source, target, send_sems, recv_sems, plane):
        def one(i, _):
            other = plane * members + lax.rem(my_place + i, members)

            @pl.when(other != me)
            def _wait():
                copy(source, target, send_sems, recv_sems, other, other).wait_recv()

            return _

        lax.fori_loop(0, members, one, 0)

    def dispatch(step, _):
        plane = plane_out(step)
        picked = lax.dot_general(
            spread[plane],
            mixed[...],
            (((0,), (0,)), ((), ())),
            preferred_element_type=jnp.float32,
        ).astype(jnp.bfloat16)
        pack(picked, sent, plane)
        send_plane(sent, got, sent_sems, got_sems, plane)
        return _

    lax.fori_loop(0, planes, dispatch, 0)

    for load in loads:
        load.wait()

    tile = min(256, hidden_width)
    down_tile = min(512, width)

    def experts(step, _):
        plane = plane_in(step)
        await_plane(sent, got, sent_sems, got_sems, plane)
        stack[...] = unpack(got, plane)
        for c in range(pieces):
            rows[:, c * piece : (c + 1) * piece] = stack[c * plane_rows : (c + 1) * plane_rows, :]

        def hide(j, _):
            part = pl.ds(pl.multiple_of(j * tile, tile), tile)
            gate_part = dot(rows[...], gate_ref[:, part])
            up_part = dot(rows[...], up_ref[:, part])
            value = gate_part / (1.0 + jnp.exp(-gate_part)) * up_part
            hidden[:, part] = value.astype(jnp.bfloat16)
            return _

        lax.fori_loop(0, hidden_width // tile, hide, 0)

        def lower(j, _):
            part = pl.ds(pl.multiple_of(j * down_tile, down_tile), down_tile)
            rows[:, part] = dot(hidden[...], down_ref[:, part]).astype(jnp.bfloat16)
            return _

        lax.fori_loop(0, width // down_tile, lower, 0)
        pack(rows, answer, plane)
        send_plane(answer, back, answer_sems, back_sems, plane)
        return _

    lax.fori_loop(0, planes, experts, 0)

    acc[...] = joined[...].astype(jnp.float32)

    def combine(step, _):
        plane = plane_in(step)
        await_plane(answer, back, answer_sems, back_sems, plane)
        stack[...] = unpack(back, plane)
        for c in range(pieces):
            values = stack[c * plane_rows : (c + 1) * plane_rows, :]
            cols = slice(c * piece, (c + 1) * piece)
            acc[:, cols] += dot(weight[plane, 0], values) + dot(weight[plane, 1], values)
        return _

    lax.fori_loop(0, planes, combine, 0)
    out_ref[...] = acc[...].astype(jnp.bfloat16)

    def finish(i, _):
        other = lax.rem(me + i, total)
        copy(sent, got, sent_sems, got_sems, other, me).wait_send()
        copy(answer, back, answer_sems, back_sems, other, me).wait_send()
        return _

    lax.fori_loop(1, total, finish, 0)


def body(tokens, join_weight, join_gain, moe_gain, w_gate, w_up, w_down, expert_ids, gate_scores):
    loc_count = lax.axis_size("loc")
    sensor_count = lax.axis_size("sensor")
    stream = tokens[0]
    tok_rows = stream.shape[0]
    width = stream.shape[1]
    hidden_width = w_gate.shape[3]
    top_count = expert_ids.shape[3]
    expert_total = loc_count * sensor_count
    capacity = max(2, (3 * top_count * tok_rows + 2 * expert_total - 1) // (2 * expert_total))
    planes = 4
    members = expert_total // planes
    plane_rows = members * capacity
    pieces = 16 // math.gcd(16, capacity)
    piece = width // pieces
    slab = pieces * capacity
    line = jnp.arange(members * slab, dtype=jnp.int32)
    place_of = (line // capacity) % pieces * plane_rows + line // slab * capacity + line % capacity
    pack = (place_of[:, None] == line[None, :]).astype(jnp.bfloat16)
    unpack = (line[:, None] == place_of[None, :]).astype(jnp.bfloat16)
    vmem = pl.BlockSpec(memory_space=pltpu.VMEM)
    hbm = pl.BlockSpec(memory_space=pl.ANY)
    box = pltpu.VMEM((expert_total, slab, piece), jnp.bfloat16)
    out = pl.pallas_call(
        functools.partial(kernel, (planes, members, sensor_count, pieces, capacity)),
        out_shape=jax.ShapeDtypeStruct((tok_rows, width), jnp.bfloat16),
        in_specs=[vmem] * 7 + [hbm] * 4,
        out_specs=vmem,
        scratch_shapes=[
            pltpu.VMEM((width, width), jnp.bfloat16),
            pltpu.VMEM((width, hidden_width), jnp.bfloat16),
            pltpu.VMEM((width, hidden_width), jnp.bfloat16),
            pltpu.VMEM((hidden_width, width), jnp.bfloat16),
            box,
            box,
            box,
            box,
            pltpu.VMEM((pieces * plane_rows, piece), jnp.bfloat16),
            pltpu.VMEM((plane_rows, width), jnp.bfloat16),
            pltpu.VMEM((plane_rows, hidden_width), jnp.bfloat16),
            pltpu.VMEM((tok_rows, width), jnp.float32),
            pltpu.VMEM((tok_rows, width), jnp.bfloat16),
            pltpu.VMEM((tok_rows, width), jnp.bfloat16),
            pltpu.VMEM((tok_rows, width), jnp.bfloat16),
            pltpu.VMEM((tok_rows, width), jnp.bfloat16),
            pltpu.VMEM((planes, tok_rows, plane_rows), jnp.bfloat16),
            pltpu.VMEM((planes, 2, tok_rows, plane_rows), jnp.bfloat16),
            pltpu.SemaphoreType.DMA((4,)),
            pltpu.SemaphoreType.DMA((2,)),
            pltpu.SemaphoreType.DMA((expert_total,)),
            pltpu.SemaphoreType.DMA((expert_total,)),
            pltpu.SemaphoreType.DMA((expert_total,)),
            pltpu.SemaphoreType.DMA((expert_total,)),
        ],
        compiler_params=pltpu.CompilerParams(
            collective_id=0, has_side_effects=True, vmem_limit_bytes=52 * 1024 * 1024
        ),
    )(
        stream,
        join_gain[0],
        moe_gain[0],
        expert_ids[0, 0],
        gate_scores[0, 0],
        pack,
        unpack,
        join_weight[0, 0],
        w_gate[0, 0],
        w_up[0, 0],
        w_down[0, 0],
    )
    return out[None]


def solution(mesh):
    placed = (
        P("sensor", "loc", None),
        P(None, "sensor", None, None),
        P(None, "sensor", None),
        P(None, "sensor", None),
        P(None, ("loc", "sensor"), None, None),
        P(None, ("loc", "sensor"), None, None),
        P(None, ("loc", "sensor"), None, None),
        P(None, "sensor", "loc", None),
        P(None, "sensor", "loc", None),
    )
    return jax.shard_map(
        body, mesh=mesh, in_specs=placed, out_specs=P("sensor", "loc", None), check_vma=False
    )
```

```python
import functools
import math
import jax
import jax.numpy as jnp
from jax import lax
from jax.experimental import pallas as pl
from jax.experimental.pallas import tpu as pltpu
from jax.sharding import PartitionSpec as P

MESH = pl.DeviceIdType.MESH


def norm_rows(values, gain):
    scale = lax.rsqrt(jnp.mean(values * values, axis=-1, keepdims=True) + 1e-05)
    return values * scale * gain.astype(jnp.float32)


def dot(a, b):
    return jnp.dot(a, b, preferred_element_type=jnp.float32)


def kernel(
    dims,
    stream_hbm,
    join_gain_hbm,
    moe_gain_hbm,
    ids_hbm,
    scores_hbm,
    join_hbm,
    gate_hbm,
    up_hbm,
    down_hbm,
    out_ref,
    stream_ref,
    join_gain_ref,
    moe_gain_ref,
    ids_ref,
    scores_ref,
    pack_ref,
    unpack_ref,
    join_ref,
    gate_ref,
    up_ref,
    down_ref,
    sent,
    got,
    answer,
    back,
    stack,
    rows,
    hidden,
    acc,
    normed,
    normed_in,
    joined,
    mixed,
    spread,
    weight,
    load_sems,
    swap_sems,
    sent_sems,
    got_sems,
    answer_sems,
    back_sems,
):
    planes, members, sensors, pieces, capacity = dims
    total = planes * members
    piece = stack.shape[1]
    plane_rows = rows.shape[0]
    slab = sent.shape[1]
    width = rows.shape[1]
    hidden_width = hidden.shape[1]
    me = lax.axis_index("loc") * sensors + lax.axis_index("sensor")
    my_plane = me // members
    my_place = me % members
    half = planes // 2
    my_half = my_plane // half

    def device(index):
        return (index // sensors, index % sensors)

    first_loads = [
        pltpu.make_async_copy(src, dst, load_sems.at[4 + i])
        for i, (src, dst) in enumerate(
            (
                (stream_hbm, stream_ref),
                (join_gain_hbm, join_gain_ref),
                (moe_gain_hbm, moe_gain_ref),
                (ids_hbm, ids_ref),
                (scores_hbm, scores_ref),
            )
        )
    ]
    for load in first_loads:
        load.start()
    join_load = pltpu.make_async_copy(join_hbm, join_ref, load_sems.at[3])
    join_load.start()
    loads = [
        pltpu.make_async_copy(src, dst, load_sems.at[i])
        for i, (src, dst) in enumerate(
            ((gate_hbm, gate_ref), (up_hbm, up_ref), (down_hbm, down_ref))
        )
    ]

    barrier = pltpu.get_barrier_semaphore()

    def greet(i, _):
        other = lax.rem(me + i, total)
        pl.semaphore_signal(barrier, inc=1, device_id=device(other), device_id_type=MESH)
        return _

    lax.fori_loop(1, total, greet, 0)

    for load in first_loads:
        load.wait()
    normed[...] = norm_rows(stream_ref[...].astype(jnp.float32), join_gain_ref[...]).astype(
        jnp.bfloat16
    )
    pl.semaphore_wait(barrier, total - 1)
    swap = pltpu.make_async_remote_copy(
        src_ref=normed,
        dst_ref=normed_in,
        send_sem=swap_sems.at[0],
        recv_sem=swap_sems.at[1],
        device_id=(lax.axis_index("loc"), 1 - lax.axis_index("sensor")),
        device_id_type=MESH,
    )
    swap.start()

    tok_rows = stream_ref.shape[0]
    top_count = ids_ref.shape[0]
    expert = lax.broadcasted_iota(jnp.int32, (tok_rows, total), 1)
    lower_rows = lax.broadcasted_iota(jnp.int32, (tok_rows, tok_rows), 0)
    lower_cols = lax.broadcasted_iota(jnp.int32, (tok_rows, tok_rows), 1)

    def column(line):
        square = jnp.where(lower_rows == lower_cols, line, 0.0)
        return jnp.sum(square, axis=1, keepdims=True)

    ids = [
        column(ids_ref[k : k + 1, :].astype(jnp.float32)).astype(jnp.int32)
        for k in range(top_count)
    ]
    scores = [column(scores_ref[k : k + 1, :]) for k in range(top_count)]
    chosen = [(ids[k] == expert).astype(jnp.float32) for k in range(top_count)]
    before = (lower_cols < lower_rows).astype(jnp.float32).astype(jnp.bfloat16)
    earlier = dot(before, sum(chosen).astype(jnp.bfloat16))
    position = [
        ids[k] * capacity
        + jnp.sum(earlier * chosen[k], axis=1, keepdims=True).astype(jnp.int32)
        for k in range(top_count)
    ]
    for plane in range(planes):
        slot = plane * plane_rows + lax.broadcasted_iota(jnp.int32, (tok_rows, plane_rows), 1)
        taken = [position[k] == slot for k in range(top_count)]
        spread[plane] = sum(jnp.where(t, 1.0, 0.0) for t in taken).astype(jnp.bfloat16)
        value = sum(jnp.where(taken[k], scores[k], 0.0) for k in range(top_count))
        high = value.astype(jnp.bfloat16)
        weight[plane, 0] = high
        weight[plane, 1] = (value - high.astype(jnp.float32)).astype(jnp.bfloat16)

    line_count = members * slab

    def place_of(axis):
        line = lax.broadcasted_iota(jnp.int32, (line_count, line_count), axis).astype(jnp.float32)
        member = jnp.floor((line + 0.5) * (1.0 / slab))
        inside = line - member * slab
        which = jnp.floor((inside + 0.5) * (1.0 / capacity))
        return which * plane_rows + member * capacity + (inside - which * capacity)

    for axis, target in ((0, pack_ref), (1, unpack_ref)):
        line = lax.broadcasted_iota(jnp.int32, (line_count, line_count), 1 - axis)
        target[...] = jnp.where(place_of(axis) == line.astype(jnp.float32), 1.0, 0.0).astype(
            jnp.bfloat16
        )

    swap.wait()
    join_load.wait()
    for load in loads:
        load.start()
    join_tile = min(512, width)

    def join(j, _):
        part = pl.ds(pl.multiple_of(j * join_tile, join_tile), join_tile)
        value = stream_ref[:, part].astype(jnp.float32) + dot(normed_in[...], join_ref[:, part])
        joined[:, part] = value.astype(jnp.bfloat16)
        return _

    lax.fori_loop(0, width // join_tile, join, 0)
    mixed[...] = norm_rows(joined[...].astype(jnp.float32), moe_gain_ref[...]).astype(jnp.bfloat16)

    def far(k):
        return (1 - my_half) * half + (my_plane + k) % half

    def near(k):
        return my_half * half + (my_plane + k) % half

    def plane_out(step):
        return jnp.where(step < half, far(step), near(step))

    def plane_in(step):
        return jnp.where(step % 2 == 0, near(step // 2), far(step // 2))

    def pack(values, target, plane):
        for c in range(pieces):
            stack[c * plane_rows : (c + 1) * plane_rows, :] = values[:, c * piece : (c + 1) * piece]
        packed = dot(pack_ref[...], stack[...]).astype(jnp.bfloat16)
        target[pl.ds(plane * members, members)] = packed.reshape(members, slab, piece)

    def unpack(source, plane):
        values = source[pl.ds(plane * members, members)].reshape(members * slab, piece)
        return dot(unpack_ref[...], values).astype(jnp.bfloat16)

    def copy(source, target, send_sems, recv_sems, other, landing):
        return pltpu.make_async_remote_copy(
            src_ref=source.at[other],
            dst_ref=target.at[landing],
            send_sem=send_sems.at[other],
            recv_sem=recv_sems.at[landing],
            device_id=device(other),
            device_id_type=MESH,
        )

    def send_plane(source, target, send_sems, recv_sems, plane):
        def one(i, _):
            other = plane * members + lax.rem(my_place + i, members)

            @pl.when(other != me)
            def _send():
                copy(source, target, send_sems, recv_sems, other, me).start()

            @pl.when(other == me)
            def _keep():
                target[me] = source[me]

            return _

        lax.fori_loop(0, members, one, 0)

    def await_plane(source, target, send_sems, recv_sems, plane):
        def one(i, _):
            other = plane * members + lax.rem(my_place + i, members)

            @pl.when(other != me)
            def _wait():
                copy(source, target, send_sems, recv_sems, other, other).wait_recv()

            return _

        lax.fori_loop(0, members, one, 0)

    def dispatch(step, _):
        plane = plane_out(step)
        picked = lax.dot_general(
            spread[plane],
            mixed[...],
            (((0,), (0,)), ((), ())),
            preferred_element_type=jnp.float32,
        ).astype(jnp.bfloat16)
        pack(picked, sent, plane)
        send_plane(sent, got, sent_sems, got_sems, plane)
        return _

    lax.fori_loop(0, planes, dispatch, 0)

    for load in loads:
        load.wait()

    tile = min(256, hidden_width)
    down_tile = min(512, width)

    def experts(step, _):
        plane = plane_in(step)
        await_plane(sent, got, sent_sems, got_sems, plane)
        stack[...] = unpack(got, plane)
        for c in range(pieces):
            rows[:, c * piece : (c + 1) * piece] = stack[c * plane_rows : (c + 1) * plane_rows, :]

        def hide(j, _):
            part = pl.ds(pl.multiple_of(j * tile, tile), tile)
            gate_part = dot(rows[...], gate_ref[:, part])
            up_part = dot(rows[...], up_ref[:, part])
            value = gate_part / (1.0 + jnp.exp(-gate_part)) * up_part
            hidden[:, part] = value.astype(jnp.bfloat16)
            return _

        lax.fori_loop(0, hidden_width // tile, hide, 0)

        def lower(j, _):
            part = pl.ds(pl.multiple_of(j * down_tile, down_tile), down_tile)
            rows[:, part] = dot(hidden[...], down_ref[:, part]).astype(jnp.bfloat16)
            return _

        lax.fori_loop(0, width // down_tile, lower, 0)
        pack(rows, answer, plane)
        send_plane(answer, back, answer_sems, back_sems, plane)
        return _

    lax.fori_loop(0, planes, experts, 0)

    acc[...] = joined[...].astype(jnp.float32)

    def combine(step, _):
        plane = plane_in(step)
        await_plane(answer, back, answer_sems, back_sems, plane)
        stack[...] = unpack(back, plane)
        for c in range(pieces):
            values = stack[c * plane_rows : (c + 1) * plane_rows, :]
            cols = slice(c * piece, (c + 1) * piece)
            acc[:, cols] += dot(weight[plane, 0], values) + dot(weight[plane, 1], values)
        return _

    lax.fori_loop(0, planes, combine, 0)
    out_ref[...] = acc[...].astype(jnp.bfloat16)

    def finish(i, _):
        other = lax.rem(me + i, total)
        copy(sent, got, sent_sems, got_sems, other, me).wait_send()
        copy(answer, back, answer_sems, back_sems, other, me).wait_send()
        return _

    lax.fori_loop(1, total, finish, 0)


def body(tokens, join_weight, join_gain, moe_gain, w_gate, w_up, w_down, expert_ids, gate_scores):
    loc_count = lax.axis_size("loc")
    sensor_count = lax.axis_size("sensor")
    stream = tokens[0]
    tok_rows = stream.shape[0]
    width = stream.shape[1]
    hidden_width = w_gate.shape[3]
    top_count = expert_ids.shape[3]
    expert_total = loc_count * sensor_count
    capacity = max(2, (3 * top_count * tok_rows + 2 * expert_total - 1) // (2 * expert_total))
    planes = 4
    members = expert_total // planes
    plane_rows = members * capacity
    pieces = 16 // math.gcd(16, capacity)
    piece = width // pieces
    slab = pieces * capacity
    vmem = pl.BlockSpec(memory_space=pltpu.VMEM)
    hbm = pl.BlockSpec(memory_space=pltpu.HBM)
    box = pltpu.VMEM((expert_total, slab, piece), jnp.bfloat16)
    out = pl.pallas_call(
        functools.partial(kernel, (planes, members, sensor_count, pieces, capacity)),
        out_shape=jax.ShapeDtypeStruct((tok_rows, width), jnp.bfloat16),
        in_specs=[hbm] * 9,
        out_specs=vmem,
        scratch_shapes=[
            pltpu.VMEM((tok_rows, width), jnp.bfloat16),
            pltpu.VMEM((1, width), jnp.bfloat16),
            pltpu.VMEM((1, width), jnp.bfloat16),
            pltpu.VMEM((top_count, tok_rows), jnp.int32),
            pltpu.VMEM((top_count, tok_rows), jnp.float32),
            pltpu.VMEM((members * slab, pieces * plane_rows), jnp.bfloat16),
            pltpu.VMEM((pieces * plane_rows, members * slab), jnp.bfloat16),
            pltpu.VMEM((width, width), jnp.bfloat16),
            pltpu.VMEM((width, hidden_width), jnp.bfloat16),
            pltpu.VMEM((width, hidden_width), jnp.bfloat16),
            pltpu.VMEM((hidden_width, width), jnp.bfloat16),
            box,
            box,
            box,
            box,
            pltpu.VMEM((pieces * plane_rows, piece), jnp.bfloat16),
            pltpu.VMEM((plane_rows, width), jnp.bfloat16),
            pltpu.VMEM((plane_rows, hidden_width), jnp.bfloat16),
            pltpu.VMEM((tok_rows, width), jnp.float32),
            pltpu.VMEM((tok_rows, width), jnp.bfloat16),
            pltpu.VMEM((tok_rows, width), jnp.bfloat16),
            pltpu.VMEM((tok_rows, width), jnp.bfloat16),
            pltpu.VMEM((tok_rows, width), jnp.bfloat16),
            pltpu.VMEM((planes, tok_rows, plane_rows), jnp.bfloat16),
            pltpu.VMEM((planes, 2, tok_rows, plane_rows), jnp.bfloat16),
            pltpu.SemaphoreType.DMA((9,)),
            pltpu.SemaphoreType.DMA((2,)),
            pltpu.SemaphoreType.DMA((expert_total,)),
            pltpu.SemaphoreType.DMA((expert_total,)),
            pltpu.SemaphoreType.DMA((expert_total,)),
            pltpu.SemaphoreType.DMA((expert_total,)),
        ],
        compiler_params=pltpu.CompilerParams(
            collective_id=0, has_side_effects=True, vmem_limit_bytes=52 * 1024 * 1024
        ),
    )(
        stream,
        join_gain[0],
        moe_gain[0],
        expert_ids[0, 0].T,
        gate_scores[0, 0].T,
        join_weight[0, 0],
        w_gate[0, 0],
        w_up[0, 0],
        w_down[0, 0],
    )
    return out[None]


def solution(mesh):
    placed = (
        P("sensor", "loc", None),
        P(None, "sensor", None, None),
        P(None, "sensor", None),
        P(None, "sensor", None),
        P(None, ("loc", "sensor"), None, None),
        P(None, ("loc", "sensor"), None, None),
        P(None, ("loc", "sensor"), None, None),
        P(None, "sensor", "loc", None),
        P(None, "sensor", "loc", None),
    )
    return jax.shard_map(
        body, mesh=mesh, in_specs=placed, out_specs=P("sensor", "loc", None), check_vma=False
    )
```
